512 devices in a mesh: gx: 8 (over y), gy: 8 (over z_hi, core), gz: 8 (over z_lo, x).
Axes of the slice: x: 4, y: 8, z: 8 (z_hi: 4, z_lo: 2; z = z_hi * 2 + z_lo), core: 2. Of those that a mesh axis runs over, the one named last changes fastest.
Arguments:
- stash: bfloat16 [640, 6144], P(('gy', 'gz'), 'gx'), may hold values from -16 to 16
- mlp_grad: bfloat16 [640, 6144], P(('gy', 'gz'), 'gx'), may hold values from -16 to 16
- qkv_grad: bfloat16 [640, 18432], P('gx', ('gy', 'gz')), may hold values from -16 to 16
- w_gate: bfloat16 [6144, 16384], P('gx', ('gy', 'gz')), may hold values from -0.078125 to 0.078125
- w_up: bfloat16 [6144, 16384], P('gx', ('gy', 'gz')), may hold values from -0.078125 to 0.078125
- w_down: bfloat16 [16384, 6144], P(('gy', 'gz'), 'gx'), may hold values from -0.046875 to 0.046875
- w_qkv: bfloat16 [6144, 18432], P('gx', ('gy', 'gz')), may hold values from -0.078125 to 0.078125
Outputs:
- grad_input: bfloat16 [640, 6144], P(('gy', 'gz'), 'gx')
- grad_gate: bfloat16 [6144, 16384], P('gx', ('gy', 'gz'))
- grad_up: bfloat16 [6144, 16384], P('gx', ('gy', 'gz'))
- grad_down: bfloat16 [16384, 6144], P(('gy', 'gz'), 'gx')
- grad_qkv: bfloat16 [6144, 18432], P('gx', ('gy', 'gz'))
The draws below stay inside these ranges and needn't reach their ends.
All inputs are finite; a program needn't handle non-finite values.
Results may differ from the reference program's by a relative error of at most 0.0049.
Values may be sent and summed in bfloat16 or wider, within the bound.
A program may use at most 64 MiB of HBM per device.

```python
import jax
import jax.numpy as jnp

D = 6144
FF = 16384
TOKENS = 640


def strengthened(array, key, source, target, shards_of, factor):
    def block_of(dim):
        return (jnp.arange(array.shape[dim]) // (array.shape[dim] // shards_of)).reshape((-1,) + (1,) * (array.ndim - 1 - dim))

    near = jax.random.permutation(key, shards_of)[block_of(target)]
    far = (block_of(target) + shards_of // 2) % shards_of
    return jnp.where((block_of(source) == near) | (block_of(source) == far), factor * array, array)


def levels(rng, shape, pieces, low, largest):
    loudness = 1.0
    for dim, shards_of in pieces:
        steps = jax.random.uniform(jax.random.fold_in(jax.random.fold_in(rng, 6), dim), (shards_of,), jnp.float32, low / len(pieces), largest / len(pieces))
        loudness = loudness * jnp.repeat(jnp.exp(steps), shape[dim] // shards_of).reshape((-1,) + (1,) * (len(shape) - 1 - dim))
    return loudness


def centred(rng, extent, scale, most, pieces=(), dtype=jnp.bfloat16):
    drawn = jax.random.normal(rng, extent, jnp.float32) * scale
    if len(pieces) > 0:
        drawn = levels(rng, extent, pieces, -0.22, 0.18) * drawn
    return jnp.clip(drawn, min=-most, max=most).astype(dtype)


def noise_with(key, dims, scale, bound, cuts, heavy, dtype=jnp.bfloat16):
    entries = scale * jax.random.normal(key, dims, jnp.float32)
    if cuts:
        entries = entries * levels(key, dims, cuts, -0.22, 0.18)
    return jnp.clip(strengthened(entries, jax.random.fold_in(key, 3), *heavy), -bound, bound).astype(dtype)


def setup_inputs(seed: int = 0) -> dict:
    key_list = jax.random.split(jax.random.key(seed), 8)
    return {
        "stash": noise_with(key_list[0], (TOKENS, D), 1.0, 16.0, ((0, 64), (1, 8)), (1, 0, 64, 4.0)),
        "mlp_grad": noise_with(key_list[1], (TOKENS, D), 1.0, 16.0, ((0, 64), (1, 8)), (1, 0, 64, 4.0)),
        "qkv_grad": noise_with(key_list[2], (TOKENS, 3 * D), 1.0, 16.0, ((0, 8), (1, 64)), (1, 0, 64, 4.0)),
        "w_gate": centred(key_list[3], (D, FF), D ** -0.5, 0.078125, ((0, 8), (1, 64))),
        "w_up": centred(key_list[4], (D, FF), D ** -0.5, 0.078125, ((0, 8), (1, 64))),
        "w_down": centred(key_list[5], (FF, D), FF ** -0.5, 0.046875, ((0, 64), (1, 8))),
        "w_qkv": centred(key_list[6], (D, 3 * D), D ** -0.5, 0.078125, ((0, 8), (1, 64))),
    }


def reference(stash, mlp_grad, qkv_grad, w_gate, w_up, w_down, w_qkv):
    gate = jnp.dot(stash, w_gate, preferred_element_type=jnp.float32)
    up = jnp.dot(stash, w_up, preferred_element_type=jnp.float32)
    hidden_grad = jnp.dot(mlp_grad, w_down.T, preferred_element_type=jnp.float32)
    sigmoid_gate = jax.nn.sigmoid(gate)
    activated = gate * sigmoid_gate
    hidden = (activated * up).astype(jnp.bfloat16)
    d_gate = (hidden_grad * up * sigmoid_gate * (1.0 + gate * (1.0 - sigmoid_gate))).astype(jnp.bfloat16)
    d_up = (hidden_grad * activated).astype(jnp.bfloat16)
    grad_down = jnp.dot(hidden.T, mlp_grad, preferred_element_type=jnp.float32).astype(jnp.bfloat16)
    grad_gate = jnp.dot(stash.T, d_gate, preferred_element_type=jnp.float32).astype(jnp.bfloat16)
    grad_up = jnp.dot(stash.T, d_up, preferred_element_type=jnp.float32).astype(jnp.bfloat16)
    grad_qkv = jnp.dot(stash.T, qkv_grad, preferred_element_type=jnp.float32).astype(jnp.bfloat16)
    summed = jnp.dot(d_gate, w_gate.T, preferred_element_type=jnp.float32)
    summed = summed + jnp.dot(d_up, w_up.T, preferred_element_type=jnp.float32)
    summed = summed + jnp.dot(qkv_grad, w_qkv.T, preferred_element_type=jnp.float32)
    grad_input = summed.astype(jnp.bfloat16)
    return (grad_input, grad_gate, grad_up, grad_down, grad_qkv)
```

```python
import jax
import jax.numpy as jnp
from jax import lax
from jax.experimental import pallas as pl
from jax.experimental.pallas import tpu as pltpu
from jax.sharding import PartitionSpec as P

MESH = pl.DeviceIdType.MESH
F32 = jnp.float32
BF16 = jnp.bfloat16
NY = 8
NS = 8
NH = 4
ROWS = 10
PAD = 16
BLK = 80
TB = 40
LANES = 128


def nt(left, right):
    return lax.dot_general(left, right, (((1,), (1,)), ((), ())), preferred_element_type=F32)


def tn(left, right):
    return lax.dot_general(left, right, (((0,), (0,)), ((), ())), preferred_element_type=F32)


def packing(shape, padded_dim):
    padded = lax.broadcasted_iota(jnp.int32, shape, padded_dim)
    packed = lax.broadcasted_iota(jnp.int32, shape, 1 - padded_dim)
    shard = lax.shift_right_logical(padded, 4)
    row = padded - shard * PAD
    return jnp.where((row < ROWS) & (packed == shard * ROWS + row), 1.0, 0.0).astype(BF16)


def kernel(
    stash, mlp, qkv, wg, wu, wd, wq,
    gi_out, gg_out, gu_out, gd_out, gq_out,
    pad, zin, shards, xs, xm, q, pf, sb, rb, ab, hid, dg, du, gif, cr, rs1, rr1, z2, zr,
    z_ss, z_rs, g_ss, g_rs, x_ss, x_rs, q_ss, q_rs, s_ss, s_rs, a_ss, a_rs, c_ss, c_rs, r_ss, r_rs, e_ss, e_rs,
):
    y = lax.axis_index("gx")
    gy = lax.axis_index("gy")
    s = lax.axis_index("gz")
    core, hi = gy % 2, gy // 2
    lo, x = s // 4, s % 4

    def at_y(d):
        return ((y + d) % NY, gy, s)

    def shard_peer(r):
        return ((lo + r // 4) % 2) * 4 + (x + r % 4) % 4

    def at_s(r):
        return (y, gy, shard_peer(r))

    def at_hi(k):
        return (y, ((hi + k + NH) % NH) * 2 + core, s)

    sibling = (y, hi * 2 + (1 - core), s)

    sends = []

    def send(src, dst, ss, rs, device):
        copy = pltpu.make_async_remote_copy(
            src_ref=src, dst_ref=dst, send_sem=ss, recv_sem=rs, device_id=device, device_id_type=MESH
        )
        copy.start()
        sends.append(copy)
        return copy

    pad[...] = jnp.zeros_like(pad)
    pad[0:ROWS, :] = stash[...]
    pad[PAD : PAD + ROWS, :] = mlp[...]
    shards[0, s] = pad[...]
    q[y] = qkv[...]

    barrier = pltpu.get_barrier_semaphore()
    partners = [at_y(d) for d in range(1, NY)] + [at_s(r) for r in range(1, NS)]
    partners += [at_hi(k) for k in range(1, NH)] + [sibling]
    for device in partners:
        pl.semaphore_signal(barrier, inc=1, device_id=device, device_id_type=MESH)
    pl.semaphore_wait(barrier, len(partners))

    def spread(k, src):
        return [
            send(src, shards.at[k, s], g_ss.at[k, r], g_rs.at[k, r], at_s(r))
            for r in (6, 2, 5, 7, 1, 3, 4)
        ]

    shard_copies = {0: spread(0, pad)}
    z_copies = {
        k: send(pad, zin.at[k], z_ss.at[k], z_rs.at[k], at_hi(-k)) for k in (2, 1, 3)
    }
    q_copies = [send(qkv, q.at[y], q_ss.at[d], q_rs.at[d], at_y(d)) for d in (4, 3, 5, 2, 6, 1, 7)]

    def group(k):
        return ((hi + k) % NH) * 2

    def forward_shard(k):
        z_copies[k].wait_recv()
        shard_copies[k] = spread(k, zin.at[k])
        shards[k, s] = zin[k]

    swaps = {}

    def gather_rows(k):
        for copy in shard_copies[k]:
            copy.wait_recv()
        pack = packing((BLK, NS * PAD), 1)
        block = group(k) + core
        for i, out in enumerate((xs, xm)):
            rows = shards[k, :, i * PAD : (i + 1) * PAD, :].reshape(NS * PAD, -1)
            out[block] = jnp.dot(pack, rows, preferred_element_type=F32).astype(BF16)
        swaps[k] = [
            send(out.at[block], out.at[block], x_ss.at[k, i], x_rs.at[k, i], sibling)
            for i, out in enumerate((xs, xm))
        ]

    sums = {}

    def project(k):
        for copy in swaps[k]:
            copy.wait_recv()
        rows = xs[pl.ds(group(k), 2)].reshape(2 * BLK, -1)
        grads = xm[pl.ds(group(k), 2)].reshape(2 * BLK, -1)
        gate = jnp.dot(rows, wg[...], preferred_element_type=F32)
        up = jnp.dot(rows, wu[...], preferred_element_type=F32)
        back = nt(grads, wd[...])
        for owner in range(NY):
            tb, ch = owner // 2, owner % 2
            part = jnp.concatenate(
                [
                    a[tb * TB : (tb + 1) * TB, ch * LANES : (ch + 1) * LANES]
                    for a in (gate, up, back)
                ]
                + [jnp.zeros((LANES - 3 * TB, LANES), F32)],
                axis=0,
            )
            pf[k, owner] = part
            sb[k, owner] = part.astype(BF16)
        sums[k] = [
            send(sb.at[k, (y + d) % NY], rb.at[k, d], s_ss.at[k, d], s_rs.at[k, d], at_y(d))
            for d in (4, 3, 5, 2, 6, 1, 7)
        ]

    results = {}

    def elementwise(k):
        total = pf[k, y]
        for copy in sums[k]:
            copy.wait_recv()
        for d in range(1, NY):
            total = total + rb[k, d].astype(F32)
        gate, up, back = total[0:TB], total[TB : 2 * TB], total[2 * TB : 3 * TB]
        sig = jax.nn.sigmoid(gate)
        act = gate * sig
        out = jnp.concatenate(
            [
                act * up,
                back * up * sig * (1.0 + gate * (1.0 - sig)),
                back * act,
                jnp.zeros((LANES - 3 * TB, LANES), F32),
            ],
            axis=0,
        )
        ab[k, y] = out.astype(BF16)
        results[k] = [
            send(ab.at[k, y], ab.at[k, y], a_ss.at[k, d], a_rs.at[k, d], at_y(d))
            for d in (4, 3, 5, 2, 6, 1, 7)
        ]

    halves = {}

    def input_partial(k):
        for copy in results[k]:
            copy.wait_recv()
        if k == 0:
            for copy in q_copies:
                copy.wait_recv()
        for b in range(2):
            for ch in range(2):
                first = ab[k, 4 * b + ch].astype(F32)
                second = ab[k, 4 * b + 2 + ch].astype(F32)
                for i, out in enumerate((hid, dg, du)):
                    out[group(k) + b, :, ch * LANES : (ch + 1) * LANES] = jnp.concatenate(
                        [first[i * TB : (i + 1) * TB], second[i * TB : (i + 1) * TB]], axis=0
                    ).astype(BF16)
        blocks = pl.ds(group(k), 2)
        part = nt(dg[blocks].reshape(2 * BLK, -1), wg[...])
        part += nt(du[blocks].reshape(2 * BLK, -1), wu[...])
        part += nt(q[blocks].reshape(2 * BLK, -1), wq[...])
        gif[k] = part.reshape(2, BLK, -1)
        halves[k] = send(gif.at[k, 1 - core], cr.at[k], c_ss.at[k], c_rs.at[k], sibling)

    pieces = {}

    def scatter_input(k):
        halves[k].wait_recv()
        block = (gif[k, core] + cr[k]).astype(BF16)
        unpack = packing((NS * PAD, BLK), 0)
        rs1[k] = (
            jnp.dot(unpack, block, preferred_element_type=F32).astype(BF16).reshape(NS, PAD, -1)
        )
        pieces[k] = [
            send(rs1.at[k, shard_peer(r)], rr1.at[k, r], r_ss.at[k, r], r_rs.at[k, r], at_s(r))
            for r in (6, 2, 5, 7, 1, 3, 4)
        ]

    ends = []

    def reduce_input(k):
        total = rs1[k, s].astype(F32)
        for copy in pieces[k]:
            copy.wait_recv()
        for r in range(1, NS):
            total = total + rr1[k, r].astype(F32)
        z2[k] = total
        if k > 0:
            ends.append(send(z2.at[k], zr.at[k], e_ss.at[k], e_rs.at[k], at_hi(k)))

    def flat(ref):
        return ref[...].reshape(NY * BLK, -1)

    forward_shard(1)
    gather_rows(0)
    forward_shard(2)
    project(0)
    forward_shard(3)
    gather_rows(1)
    project(1)
    elementwise(0)
    gather_rows(2)
    project(2)
    elementwise(1)
    gather_rows(3)
    project(3)
    input_partial(0)
    elementwise(2)
    scatter_input(0)
    input_partial(1)
    elementwise(3)
    scatter_input(1)
    reduce_input(0)
    input_partial(2)
    scatter_input(2)
    reduce_input(1)
    input_partial(3)
    scatter_input(3)
    reduce_input(2)
    gg_out[...] = tn(flat(xs), flat(dg)).astype(BF16)
    gu_out[...] = tn(flat(xs), flat(du)).astype(BF16)
    reduce_input(3)
    gd_out[...] = tn(flat(hid), flat(xm)).astype(BF16)
    gq_out[...] = tn(flat(xs), flat(q)).astype(BF16)
    total = z2[0]
    for copy in ends:
        copy.wait_recv()
    for k in range(1, NH):
        total = total + zr[k]
    gi_out[...] = total[0:ROWS].astype(BF16)
    for copy in sends:
        copy.wait_send()


def on_device(stash, mlp_grad, qkv_grad, w_gate, w_up, w_down, w_qkv):
    width = stash.shape[1]
    units = w_gate.shape[1]
    proj = w_qkv.shape[1]
    vmem = pl.BlockSpec(memory_space=pltpu.VMEM)
    dma = pltpu.SemaphoreType.DMA
    return pl.pallas_call(
        kernel,
        out_shape=(
            jax.ShapeDtypeStruct(stash.shape, BF16),
            jax.ShapeDtypeStruct(w_gate.shape, BF16),
            jax.ShapeDtypeStruct(w_up.shape, BF16),
            jax.ShapeDtypeStruct(w_down.shape, BF16),
            jax.ShapeDtypeStruct(w_qkv.shape, BF16),
        ),
        in_specs=[vmem] * 7,
        out_specs=(vmem,) * 5,
        scratch_shapes=[
            pltpu.VMEM((2 * PAD, width), BF16),
            pltpu.VMEM((NH, 2 * PAD, width), BF16),
            pltpu.VMEM((NH, NS, 2 * PAD, width), BF16),
            pltpu.VMEM((NY, BLK, width), BF16),
            pltpu.VMEM((NY, BLK, width), BF16),
            pltpu.VMEM((NY, BLK, proj), BF16),
            pltpu.VMEM((NH, NY, LANES, LANES), F32),
            pltpu.VMEM((NH, NY, LANES, LANES), BF16),
            pltpu.VMEM((NH, NY, LANES, LANES), BF16),
            pltpu.VMEM((NH, NY, LANES, LANES), BF16),
            pltpu.VMEM((NY, BLK, units), BF16),
            pltpu.VMEM((NY, BLK, units), BF16),
            pltpu.VMEM((NY, BLK, units), BF16),
            pltpu.VMEM((NH, 2, BLK, width), F32),
            pltpu.VMEM((NH, BLK, width), F32),
            pltpu.VMEM((NH, NS, PAD, width), BF16),
            pltpu.VMEM((NH, NS, PAD, width), BF16),
            pltpu.VMEM((NH, PAD, width), F32),
            pltpu.VMEM((NH, PAD, width), F32),
        ]
        + [dma((NH,))] * 2
        + [dma((NH, NS))] * 2
        + [dma((NH, 2))] * 2
        + [dma((NY,))] * 2
        + [dma((NH, NY))] * 2
        + [dma((NH, NY))] * 2
        + [dma((NH,))] * 2
        + [dma((NH, NS))] * 2
        + [dma((NH,))] * 2,
        compiler_params=pltpu.CompilerParams(
            collective_id=0, has_side_effects=True, vmem_limit_bytes=44 * 2**20
        ),
        cost_estimate=pl.CostEstimate(
            flops=2_600_000_000, bytes_accessed=4_000_000, transcendentals=200_000
        ),
        name="block_backward",
    )(stash, mlp_grad, qkv_grad, w_gate, w_up, w_down, w_qkv)


def solution(mesh):
    rows = P(("gy", "gz"), "gx")
    columns = P("gx", ("gy", "gz"))
    return jax.shard_map(
        on_device,
        mesh=mesh,
        in_specs=(rows, rows, columns, columns, columns, rows, columns),
        out_specs=(rows, columns, columns, rows, columns),
        check_vma=False,
    )
```

```python
import jax
import jax.numpy as jnp
from jax import lax
from jax.experimental import pallas as pl
from jax.experimental.pallas import tpu as pltpu
from jax.sharding import PartitionSpec as P

MESH = pl.DeviceIdType.MESH
F32 = jnp.float32
BF16 = jnp.bfloat16
NY = 8
NS = 8
NH = 4
ROWS = 10
PAD = 16
BLK = 80
TB = 40
LANES = 128


def nt(left, right):
    return lax.dot_general(left, right, (((1,), (1,)), ((), ())), preferred_element_type=F32)


def tn(left, right):
    return lax.dot_general(left, right, (((0,), (0,)), ((), ())), preferred_element_type=F32)


def one_hot(rows, cols, hit):
    row = lax.broadcasted_iota(jnp.int32, (rows, cols), 0)
    col = lax.broadcasted_iota(jnp.int32, (rows, cols), 1)
    return jnp.where(hit(row, col), 1.0, 0.0).astype(BF16)


def spreading(row, col):
    shard = lax.shift_right_logical(row, 4)
    token = row - shard * PAD
    return (token < ROWS) & (col == shard * ROWS + token)


def exact(left, right):
    return jnp.dot(left, right, preferred_element_type=F32)


HEAD = PAD - ROWS
TAIL = ROWS - HEAD


def pack_shard(padded, width):
    main = one_hot(PAD, 2 * PAD, lambda r, c: ((r < ROWS) & (c == r)) | ((r >= ROWS) & (c == r + HEAD)))
    parts = [exact(main, padded)]
    for half in range(2):
        part = jnp.zeros((PAD, LANES), F32)
        for i in range(4 * half, min(4 * half + 4, width // LANES)):
            low = TAIL * (i % 4)
            pick = one_hot(
                PAD, 2 * PAD, lambda r, c: (r >= low) & (r < low + TAIL) & (c == r - low + PAD + HEAD)
            )
            part += exact(pick, padded[:, i * LANES : (i + 1) * LANES])
        parts.append(part)
    return jnp.concatenate(parts, axis=1).astype(BF16)


def unpack_shards(packed, width):
    def place(row, col, low, count, start):
        shard = lax.shift_right_logical(col, 4)
        t = col - shard * PAD - low
        return (t >= 0) & (t < count) & (row == shard * ROWS + start + t)

    wide = packed[:, :width]
    rows = exact(one_hot(BLK, NS * PAD, lambda r, c: place(r, c, 0, ROWS, 0)), wide)
    grads = exact(one_hot(BLK, NS * PAD, lambda r, c: place(r, c, ROWS, HEAD, 0)), wide)
    tails = []
    for i in range(width // LANES):
        pick = one_hot(BLK, NS * PAD, lambda r, c: place(r, c, TAIL * (i % 4), TAIL, HEAD))
        first = width + LANES * (i // 4)
        tails.append(exact(pick, packed[:, first : first + LANES]))
    grads += jnp.concatenate(tails, axis=1)
    return rows.astype(BF16), grads.astype(BF16)


def kernel(
    stash_in, mlp_in, qkv_in, wg_in, wu_in, wd_in, wq_in,
    gi_out, gg_out, gu_out, gd_out, gq_out,
    stash, mlp, qkv, wg, wu, wd, wq,
    pad, packed, zin, shards, xs, xm, q, pf, sb, rb, cb, ab, hid, dg, du, gif, cr, rs1, rr1, own, z2, zr,
    w_sem, z_ss, z_rs, g_ss, g_rs, x_ss, x_rs, q_ss, q_rs, s_ss, s_rs, a_ss, a_rs, c_ss, c_rs, r_ss, r_rs, e_ss, e_rs,
):
    y = lax.axis_index("gx")
    gy = lax.axis_index("gy")
    s = lax.axis_index("gz")
    core, hi = gy % 2, gy // 2
    lo, x = s // 4, s % 4

    def at_y(d):
        return ((y + d + NY) % NY, gy, s)

    def shard_peer(r):
        return ((lo + r // 4) % 2) * 4 + (x + r % 4) % 4

    def at_s(r):
        return (y, gy, shard_peer(r))

    def at_hi(k):
        return (y, ((hi + k + NH) % NH) * 2 + core, s)

    sibling = (y, hi * 2 + (1 - core), s)

    sends = []

    def send(src, dst, ss, rs, device):
        copy = pltpu.make_async_remote_copy(
            src_ref=src, dst_ref=dst, send_sem=ss, recv_sem=rs, device_id=device, device_id_type=MESH
        )
        copy.start()
        sends.append(copy)
        return copy

    inputs = [
        pltpu.make_async_copy(src, dst, w_sem.at[i])
        for i, (src, dst) in enumerate(
            (
                (stash_in, stash),
                (mlp_in, mlp),
                (qkv_in, qkv),
                (wg_in, wg),
                (wu_in, wu),
                (wd_in, wd),
                (wq_in, wq),
            )
        )
    ]
    for copy in inputs:
        copy.start()
    barrier = pltpu.get_barrier_semaphore()
    partners = [at_y(d) for d in (1, -1, 2, -2)] + [at_s(r) for r in range(1, NS)]
    partners += [at_hi(k) for k in range(1, NH)] + [sibling]
    for device in partners:
        pl.semaphore_signal(barrier, inc=1, device_id=device, device_id_type=MESH)

    for copy in inputs[:3]:
        copy.wait()
    pad[...] = jnp.zeros_like(pad)
    pad[0:ROWS, :] = stash[...]
    pad[PAD : PAD + ROWS, :] = mlp[...]
    packed[...] = pack_shard(pad[...], stash.shape[1])
    shards[0, s] = packed[...]
    q[y] = qkv[...]

    pl.semaphore_wait(barrier, len(partners))

    def spread(k, src):
        return [
            send(src, shards.at[k, s], g_ss.at[k, r], g_rs.at[k, r], at_s(r))
            for r in (6, 2, 5, 7, 1, 3, 4)
        ]

    shard_copies = {0: spread(0, packed)}
    z_copies = {
        k: send(packed, zin.at[k], z_ss.at[k], z_rs.at[k], at_hi(-k)) for k in (2, 1, 3)
    }

    def wrap(d):
        return (y + d + NY) % NY

    def share(ref, ss, rs):
        block = ref.at[y]
        return {
            d: send(block, block, ss.at[i], rs.at[i], at_y(-d))
            for i, d in enumerate((2, -2, 1, -1))
        }

    def pass_on(copies, ref, ss, rs, cut):
        halves = {2: pl.ds(0, cut), -2: pl.ds(cut, ref.shape[1] - cut)}
        for i, d in enumerate((2, -2)):
            copies[d].wait_recv()
            block = ref.at[wrap(d)]
            part = ref.at[wrap(d), halves[d]]
            sign = d // 2
            copies[2 * d] = send(part, part, ss.at[4 + i], rs.at[4 + i], at_y(-d))
            copies[d + sign] = send(block, block, ss.at[6 + i], rs.at[6 + i], at_y(-sign))

    def shared(copies):
        for d in (1, -1, 3, -3, 4, -4):
            copies[d].wait_recv()

    q_copies = share(q, q_ss, q_rs)

    def pass_q():
        pass_on(q_copies, q, q_ss, q_rs, 48)

    def group(k):
        return ((hi + k) % NH) * 2

    def forward_shard(k):
        z_copies[k].wait_recv()
        shard_copies[k] = spread(k, zin.at[k])
        shards[k, s] = zin[k]

    swaps = {}

    def gather_rows(k):
        for copy in shard_copies[k]:
            copy.wait_recv()
        block = group(k) + core
        xs[block], xm[block] = unpack_shards(shards[k].reshape(NS * PAD, -1), stash.shape[1])
        swaps[k] = [
            send(out.at[block], out.at[block], x_ss.at[k, i], x_rs.at[k, i], sibling)
            for i, out in enumerate((xs, xm))
        ]

    sums = {}

    def project(k):
        for copy in swaps[k]:
            copy.wait_recv()
        if k == 0:
            for copy in inputs[3:6]:
                copy.wait()
        rows = xs[pl.ds(group(k), 2)].reshape(2 * BLK, -1)
        grads = xm[pl.ds(group(k), 2)].reshape(2 * BLK, -1)
        gate = jnp.dot(rows, wg[...], preferred_element_type=F32)
        up = jnp.dot(rows, wu[...], preferred_element_type=F32)
        back = nt(grads, wd[...])
        for owner in range(NY):
            tb, ch = owner // 2, owner % 2
            part = jnp.concatenate(
                [
                    a[tb * TB : (tb + 1) * TB, ch * LANES : (ch + 1) * LANES]
                    for a in (gate, up, back)
                ]
                + [jnp.zeros((LANES - 3 * TB, LANES), F32)],
                axis=0,
            )
            pf[k, owner] = part
            sb[k, owner] = part.astype(BF16)
        half = {1: pl.ds(0, LANES // 2), -1: pl.ds(LANES // 2, LANES // 2)}
        sums[k] = {}
        for slot, (dist, hop) in enumerate(((4, 2), (3, 1), (1, 1))):
            for side, sign in enumerate((1, -1)):
                src = sb.at[k, wrap(sign * dist)]
                dst = rb.at[k, 2 * slot + side]
                if dist == 4:
                    src = sb.at[k, wrap(sign * dist), half[sign]]
                    dst = rb.at[k, 2 * slot + side, half[sign]]
                n = 2 * slot + side
                sums[k][dist, sign] = send(src, dst, s_ss.at[k, n], s_rs.at[k, n], at_y(sign * hop))

    def combine(k):
        for side, sign in enumerate((1, -1)):
            sums[k][4, sign].wait_recv()
            sums[k][3, sign].wait_recv()
            rows = LANES // 2 * side
            part = pf[k, wrap(2 * sign)] + rb[k, 2 + side].astype(F32)
            far = rb[k, side, rows : rows + LANES // 2, :].astype(F32)
            blank = jnp.zeros_like(far)
            part += jnp.concatenate([far, blank] if side == 0 else [blank, far], axis=0)
            cb[k, side] = part.astype(BF16)
            sums[k][2, sign] = send(
                cb.at[k, side], rb.at[k, 6 + side], s_ss.at[k, 6 + side], s_rs.at[k, 6 + side], at_y(2 * sign)
            )

    results = {}

    def elementwise(k):
        total = pf[k, y]
        for slot, dist in ((2, 1), (3, 2)):
            for side, sign in enumerate((1, -1)):
                sums[k][dist, sign].wait_recv()
                total = total + rb[k, 2 * slot + side].astype(F32)
        gate, up, back = total[0:TB], total[TB : 2 * TB], total[2 * TB : 3 * TB]
        sig = jax.nn.sigmoid(gate)
        act = gate * sig
        out = jnp.concatenate(
            [
                act * up,
                back * up * sig * (1.0 + gate * (1.0 - sig)),
                back * act,
                jnp.zeros((LANES - 3 * TB, LANES), F32),
            ],
            axis=0,
        )
        ab[k, y] = out.astype(BF16)
        results[k] = share(ab.at[k], a_ss.at[k], a_rs.at[k])

    def pass_results(k):
        pass_on(results[k], ab.at[k], a_ss.at[k], a_rs.at[k], LANES // 2)

    halves = {}

    def input_partial(k):
        shared(results[k])
        if k == 0:
            shared(q_copies)
            inputs[6].wait()
        for b in range(2):
            for ch in range(2):
                first = ab[k, 4 * b + ch].astype(F32)
                second = ab[k, 4 * b + 2 + ch].astype(F32)
                for i, out in enumerate((hid, dg, du)):
                    out[group(k) + b, :, ch * LANES : (ch + 1) * LANES] = jnp.concatenate(
                        [first[i * TB : (i + 1) * TB], second[i * TB : (i + 1) * TB]], axis=0
                    ).astype(BF16)
        def partial(block):
            part = nt(dg[block], wg[...])
            part += nt(du[block], wu[...])
            part += jnp.dot(q[block], wq[...], preferred_element_type=F32)
            return part

        gif[k, 1] = partial(group(k) + 1 - core)
        halves[k] = send(gif.at[k, 1], cr.at[k], c_ss.at[k], c_rs.at[k], sibling)
        gif[k, 0] = partial(group(k) + core)

    pieces = {}

    def scatter_input(k):
        halves[k].wait_recv()
        block = (gif[k, 0] + cr[k]).astype(BF16)
        unpack = one_hot(NS * PAD, BLK, spreading)
        rs1[k] = (
            jnp.dot(unpack, block, preferred_element_type=F32).astype(BF16).reshape(NS, PAD, -1)
        )
        pieces[k] = [
            send(rs1.at[k, shard_peer(r)], rr1.at[k, r], r_ss.at[k, r], r_rs.at[k, r], at_s(r))
            for r in (6, 2, 5, 7, 1, 3, 4)
        ]

    ends = []

    def reduce_input(k):
        total = rs1[k, s].astype(F32)
        for copy in pieces[k]:
            copy.wait_recv()
        for r in range(1, NS):
            total = total + rr1[k, r].astype(F32)
        if k == 0:
            own[...] = total
        else:
            z2[k] = total.astype(BF16)
            ends.append(send(z2.at[k], zr.at[k], e_ss.at[k], e_rs.at[k], at_hi(k)))

    def flat(ref):
        return ref[...].reshape(NY * BLK, -1)

    gather_rows(0)
    forward_shard(1)
    pass_q()
    project(0)
    forward_shard(2)
    gather_rows(1)
    combine(0)
    project(1)
    forward_shard(3)
    elementwise(0)
    combine(1)
    gather_rows(2)
    project(2)
    pass_results(0)
    elementwise(1)
    combine(2)
    gather_rows(3)
    project(3)
    input_partial(0)
    pass_results(1)
    elementwise(2)
    combine(3)
    scatter_input(0)
    input_partial(1)
    pass_results(2)
    elementwise(3)
    scatter_input(1)
    reduce_input(0)
    input_partial(2)
    pass_results(3)
    scatter_input(2)
    reduce_input(1)
    input_partial(3)
    scatter_input(3)
    reduce_input(2)
    gg_out[...] = tn(flat(xs), flat(dg)).astype(BF16)
    gu_out[...] = tn(flat(xs), flat(du)).astype(BF16)
    reduce_input(3)
    gd_out[...] = tn(flat(hid), flat(xm)).astype(BF16)
    gq_out[...] = tn(flat(q), flat(xs)).astype(BF16)
    total = own[...]
    for copy in ends:
        copy.wait_recv()
    for k in range(1, NH):
        total = total + zr[k].astype(F32)
    gi_out[...] = total[0:ROWS].astype(BF16)
    for copy in sends:
        copy.wait_send()


def place(*refs):
    ins, outs, held = refs[:5], refs[5:10], refs[10:15]
    in_sems, out_sems = refs[15:]
    loads = [pltpu.make_async_copy(ins[i], held[i], in_sems.at[i]) for i in range(5)]
    stores = [pltpu.make_async_copy(held[i], outs[i], out_sems.at[i]) for i in range(5)]
    for copy in loads:
        copy.start()
    for load, store in zip(loads, stores):
        load.wait()
        store.start()
    for copy in stores:
        copy.wait()


def on_device(stash, mlp_grad, qkv_grad, w_gate, w_up, w_down, w_qkv):
    width = stash.shape[1]
    units = w_gate.shape[1]
    proj = w_qkv.shape[1]
    vmem = pl.BlockSpec(memory_space=pltpu.VMEM)
    hbm = pl.BlockSpec(memory_space=pltpu.HBM)
    dma = pltpu.SemaphoreType.DMA
    results = pl.pallas_call(
        kernel,
        out_shape=(
            jax.ShapeDtypeStruct(stash.shape, BF16),
            jax.ShapeDtypeStruct(w_gate.shape, BF16),
            jax.ShapeDtypeStruct(w_up.shape, BF16),
            jax.ShapeDtypeStruct(w_down.shape, BF16),
            jax.ShapeDtypeStruct((proj, width), BF16),
        ),
        in_specs=[hbm] * 7,
        out_specs=(vmem,) * 5,
        scratch_shapes=[
            pltpu.VMEM(stash.shape, BF16),
            pltpu.VMEM(mlp_grad.shape, BF16),
            pltpu.VMEM(qkv_grad.shape, BF16),
            pltpu.VMEM(w_gate.shape, BF16),
            pltpu.VMEM(w_up.shape, BF16),
            pltpu.VMEM(w_down.shape, BF16),
            pltpu.VMEM((proj, width), BF16),
            pltpu.VMEM((2 * PAD, width), BF16),
            pltpu.VMEM((PAD, width + 2 * LANES), BF16),
            pltpu.VMEM((NH, PAD, width + 2 * LANES), BF16),
            pltpu.VMEM((NH, NS, PAD, width + 2 * LANES), BF16),
            pltpu.VMEM((NY, BLK, width), BF16),
            pltpu.VMEM((NY, BLK, width), BF16),
            pltpu.VMEM((NY, BLK, proj), BF16),
            pltpu.VMEM((NH, NY, LANES, LANES), F32),
            pltpu.VMEM((NH, NY, LANES, LANES), BF16),
            pltpu.VMEM((NH, NY, LANES, LANES), BF16),
            pltpu.VMEM((NH, 2, LANES, LANES), BF16),
            pltpu.VMEM((NH, NY, LANES, LANES), BF16),
            pltpu.VMEM((NY, BLK, units), BF16),
            pltpu.VMEM((NY, BLK, units), BF16),
            pltpu.VMEM((NY, BLK, units), BF16),
            pltpu.VMEM((NH, 2, BLK, width), F32),
            pltpu.VMEM((NH, BLK, width), F32),
            pltpu.VMEM((NH, NS, PAD, width), BF16),
            pltpu.VMEM((NH, NS, PAD, width), BF16),
            pltpu.VMEM((PAD, width), F32),
            pltpu.VMEM((NH, PAD, width), BF16),
            pltpu.VMEM((NH, PAD, width), BF16),
        ]
        + [dma((7,))]
        + [dma((NH,))] * 2
        + [dma((NH, NS))] * 2
        + [dma((NH, 2))] * 2
        + [dma((NY,))] * 2
        + [dma((NH, NY))] * 2
        + [dma((NH, NY))] * 2
        + [dma((NH,))] * 2
        + [dma((NH, NS))] * 2
        + [dma((NH,))] * 2,
        compiler_params=pltpu.CompilerParams(
            collective_id=0, has_side_effects=True, vmem_limit_bytes=63 * 2**20
        ),
        cost_estimate=pl.CostEstimate(
            flops=2_600_000_000, bytes_accessed=4_000_000, transcendentals=200_000
        ),
        name="block_backward",
    )(stash, mlp_grad, qkv_grad, w_gate, w_up, w_down, w_qkv.T)
    *placed, grad_qkv = pl.pallas_call(
        place,
        out_shape=tuple(jax.ShapeDtypeStruct(a.shape, a.dtype) for a in results),
        in_specs=[hbm] * 5,
        out_specs=(hbm,) * 5,
        scratch_shapes=[pltpu.VMEM(a.shape, a.dtype) for a in results] + [dma((5,))] * 2,
        compiler_params=pltpu.CompilerParams(vmem_limit_bytes=63 * 2**20),
        name="place_results",
    )(*results)
    return (*placed, grad_qkv.T)


def solution(mesh):
    rows = P(("gy", "gz"), "gx")
    columns = P("gx", ("gy", "gz"))
    return jax.shard_map(
        on_device,
        mesh=mesh,
        in_specs=(rows, rows, columns, columns, columns, rows, columns),
        out_specs=(rows, columns, columns, rows, columns),
        check_vma=False,
    )
```

```python
import jax
import jax.numpy as jnp
from jax import lax
from jax.experimental import pallas as pl
from jax.experimental.pallas import tpu as pltpu
from jax.sharding import PartitionSpec as P

MESH = pl.DeviceIdType.MESH
F32 = jnp.float32
BF16 = jnp.bfloat16
NY = 8
NS = 8
NH = 4
ROWS = 10
PAD = 16
BLK = 80
TB = 40
LANES = 128


def nt(left, right):
    return lax.dot_general(left, right, (((1,), (1,)), ((), ())), preferred_element_type=F32)


def tn(left, right):
    return lax.dot_general(left, right, (((0,), (0,)), ((), ())), preferred_element_type=F32)


def one_hot(rows, cols, hit):
    row = lax.broadcasted_iota(jnp.int32, (rows, cols), 0)
    col = lax.broadcasted_iota(jnp.int32, (rows, cols), 1)
    return jnp.where(hit(row, col), 1.0, 0.0).astype(BF16)


def spreading(row, col):
    shard = lax.shift_right_logical(row, 4)
    token = row - shard * PAD
    return (token < ROWS) & (col == shard * ROWS + token)


def exact(left, right):
    return jnp.dot(left, right, preferred_element_type=F32)


HEAD = PAD - ROWS
TAIL = ROWS - HEAD


def pack_shard(padded, width):
    main = one_hot(PAD, 2 * PAD, lambda r, c: ((r < ROWS) & (c == r)) | ((r >= ROWS) & (c == r + HEAD)))
    parts = [exact(main, padded)]
    for half in range(2):
        part = jnp.zeros((PAD, LANES), F32)
        for i in range(4 * half, min(4 * half + 4, width // LANES)):
            low = TAIL * (i % 4)
            pick = one_hot(
                PAD, 2 * PAD, lambda r, c: (r >= low) & (r < low + TAIL) & (c == r - low + PAD + HEAD)
            )
            part += exact(pick, padded[:, i * LANES : (i + 1) * LANES])
        parts.append(part)
    return jnp.concatenate(parts, axis=1).astype(BF16)


def unpack_shards(packed, width):
    def place(row, col, low, count, start):
        shard = lax.shift_right_logical(col, 4)
        t = col - shard * PAD - low
        return (t >= 0) & (t < count) & (row == shard * ROWS + start + t)

    wide = packed[:, :width]
    rows = exact(one_hot(BLK, NS * PAD, lambda r, c: place(r, c, 0, ROWS, 0)), wide)
    grads = exact(one_hot(BLK, NS * PAD, lambda r, c: place(r, c, ROWS, HEAD, 0)), wide)
    tails = []
    for i in range(width // LANES):
        pick = one_hot(BLK, NS * PAD, lambda r, c: place(r, c, TAIL * (i % 4), TAIL, HEAD))
        first = width + LANES * (i // 4)
        tails.append(exact(pick, packed[:, first : first + LANES]))
    grads += jnp.concatenate(tails, axis=1)
    return rows.astype(BF16), grads.astype(BF16)


def kernel(
    stash_in, mlp_in, qkv_in, wg_in, wu_in, wd_in, wq_in,
    gi_hbm, gg_hbm, gu_hbm, gd_hbm, gq_hbm,
    gi_out, gg_out, gu_out, gd_out, gq_out,
    stash, mlp, qkv, wg, wu, wd, wq,
    pad, packed, zin, shards, xs, xm, q, pf, sb, rb, cb, ab, hid, dg, du, gib, gif, cr, rs1, rr1, own, z2, zr,
    w_sem, o_sem, z_ss, z_rs, g_ss, g_rs, x_ss, x_rs, q_ss, q_rs, s_ss, s_rs, a_ss, a_rs, c_ss, c_rs, r_ss, r_rs, e_ss, e_rs,
):
    y = lax.axis_index("gx")
    gy = lax.axis_index("gy")
    s = lax.axis_index("gz")
    core, hi = gy % 2, gy // 2
    lo, x = s // 4, s % 4

    def at_y(d):
        return ((y + d + NY) % NY, gy, s)

    def shard_peer(r):
        return ((lo + r // 4) % 2) * 4 + (x + r % 4) % 4

    def at_s(r):
        return (y, gy, shard_peer(r))

    def at_hi(k):
        return (y, ((hi + k + NH) % NH) * 2 + core, s)

    sibling = (y, hi * 2 + (1 - core), s)

    sends = []
    stores = []

    def send(src, dst, ss, rs, device):
        copy = pltpu.make_async_remote_copy(
            src_ref=src, dst_ref=dst, send_sem=ss, recv_sem=rs, device_id=device, device_id_type=MESH
        )
        copy.start()
        sends.append(copy)
        return copy

    inputs = [
        pltpu.make_async_copy(src, dst, w_sem.at[i])
        for i, (src, dst) in enumerate(
            (
                (stash_in, stash),
                (mlp_in, mlp),
                (qkv_in, qkv),
                (wg_in, wg),
                (wu_in, wu),
                (wd_in, wd),
                (wq_in, wq),
            )
        )
    ]
    barrier = pltpu.get_barrier_semaphore()
    partners = [at_y(d) for d in (1, -1, 2, -2)] + [at_s(r) for r in range(1, NS)]
    partners += [at_hi(k) for k in range(1, NH)] + [sibling]
    for device in partners:
        pl.semaphore_signal(barrier, inc=1, device_id=device, device_id_type=MESH)

    for copy in inputs:
        copy.start()
    for copy in inputs[:3]:
        copy.wait()
    pad[...] = jnp.zeros_like(pad)
    pad[0:ROWS, :] = stash[...]
    pad[PAD : PAD + ROWS, :] = mlp[...]
    packed[...] = pack_shard(pad[...], stash.shape[1])
    shards[0, s] = packed[...]
    q[y] = qkv[...]

    pl.semaphore_wait(barrier, len(partners))

    def spread(k, src):
        return [
            send(src, shards.at[k, s], g_ss.at[k, r], g_rs.at[k, r], at_s(r))
            for r in (6, 2, 5, 7, 1, 3, 4)
        ]

    shard_copies = {0: spread(0, packed)}
    z_copies = {
        k: send(packed, zin.at[k], z_ss.at[k], z_rs.at[k], at_hi(-k)) for k in (1, 3, 2)
    }

    def wrap(d):
        return (y + d + NY) % NY

    def share(ref, ss, rs):
        block = ref.at[y]
        return {
            d: send(block, block, ss.at[i], rs.at[i], at_y(-d))
            for i, d in enumerate((2, -2, 1, -1))
        }

    def pass_on(copies, ref, ss, rs, cut):
        halves = {2: pl.ds(0, cut), -2: pl.ds(cut, ref.shape[1] - cut)}
        for i, d in enumerate((2, -2)):
            copies[d].wait_recv()
            block = ref.at[wrap(d)]
            part = ref.at[wrap(d), halves[d]]
            sign = d // 2
            copies[2 * d] = send(part, part, ss.at[4 + i], rs.at[4 + i], at_y(-d))
            copies[d + sign] = send(block, block, ss.at[6 + i], rs.at[6 + i], at_y(-sign))

    def shared(copies):
        for d in (1, -1, 3, -3, 4, -4):
            copies[d].wait_recv()

    q_copies = share(q, q_ss, q_rs)

    def pass_q():
        pass_on(q_copies, q, q_ss, q_rs, 48)

    def group(k):
        return ((hi + k) % NH) * 2

    def forward_shard(k):
        z_copies[k].wait_recv()
        shard_copies[k] = spread(k, zin.at[k])
        shards[k, s] = zin[k]

    swaps = {}

    def gather_rows(k):
        for copy in shard_copies[k]:
            copy.wait_recv()
        block = group(k) + core
        xs[block], xm[block] = unpack_shards(shards[k].reshape(NS * PAD, -1), stash.shape[1])
        swaps[k] = [
            send(out.at[block], out.at[block], x_ss.at[k, i], x_rs.at[k, i], sibling)
            for i, out in enumerate((xs, xm))
        ]

    sums = {}

    def project(k):
        for copy in swaps[k]:
            copy.wait_recv()
        if k == 0:
            for copy in inputs[3:6]:
                copy.wait()
        rows = xs[pl.ds(group(k), 2)].reshape(2 * BLK, -1)
        grads = xm[pl.ds(group(k), 2)].reshape(2 * BLK, -1)
        gate = jnp.dot(rows, wg[...], preferred_element_type=F32)
        up = jnp.dot(rows, wu[...], preferred_element_type=F32)
        back = nt(grads, wd[...])
        for owner in range(NY):
            tb, ch = owner // 2, owner % 2
            part = jnp.concatenate(
                [
                    a[tb * TB : (tb + 1) * TB, ch * LANES : (ch + 1) * LANES]
                    for a in (gate, up, back)
                ]
                + [jnp.zeros((LANES - 3 * TB, LANES), F32)],
                axis=0,
            )
            pf[k, owner] = part
            sb[k, owner] = part.astype(BF16)
        half = {1: pl.ds(0, LANES // 2), -1: pl.ds(LANES // 2, LANES // 2)}
        sums[k] = {}
        for slot, (dist, hop) in enumerate(((4, 2), (3, 1), (1, 1))):
            for side, sign in enumerate((1, -1)):
                src = sb.at[k, wrap(sign * dist)]
                dst = rb.at[k, 2 * slot + side]
                if dist == 4:
                    src = sb.at[k, wrap(sign * dist), half[sign]]
                    dst = rb.at[k, 2 * slot + side, half[sign]]
                n = 2 * slot + side
                sums[k][dist, sign] = send(src, dst, s_ss.at[k, n], s_rs.at[k, n], at_y(sign * hop))

    def combine(k):
        for side, sign in enumerate((1, -1)):
            sums[k][4, sign].wait_recv()
            sums[k][3, sign].wait_recv()
            rows = LANES // 2 * side
            part = pf[k, wrap(2 * sign)] + rb[k, 2 + side].astype(F32)
            far = rb[k, side, rows : rows + LANES // 2, :].astype(F32)
            blank = jnp.zeros_like(far)
            part += jnp.concatenate([far, blank] if side == 0 else [blank, far], axis=0)
            cb[k, side] = part.astype(BF16)
            sums[k][2, sign] = send(
                cb.at[k, side], rb.at[k, 6 + side], s_ss.at[k, 6 + side], s_rs.at[k, 6 + side], at_y(2 * sign)
            )

    results = {}

    def elementwise(k):
        total = pf[k, y]
        for slot, dist in ((2, 1), (3, 2)):
            for side, sign in enumerate((1, -1)):
                sums[k][dist, sign].wait_recv()
                total = total + rb[k, 2 * slot + side].astype(F32)
        gate, up, back = total[0:TB], total[TB : 2 * TB], total[2 * TB : 3 * TB]
        sig = jax.nn.sigmoid(gate)
        act = gate * sig
        out = jnp.concatenate(
            [
                act * up,
                back * up * sig * (1.0 + gate * (1.0 - sig)),
                back * act,
                jnp.zeros((LANES - 3 * TB, LANES), F32),
            ],
            axis=0,
        )
        ab[k, y] = out.astype(BF16)
        results[k] = share(ab.at[k], a_ss.at[k], a_rs.at[k])

    def pass_results(k):
        pass_on(results[k], ab.at[k], a_ss.at[k], a_rs.at[k], LANES // 2)

    def project_grad():
        gq_out[...] = tn(flat(q), flat(xs)).astype(BF16)
        early = pltpu.make_async_copy(gq_out, gq_hbm, o_sem.at[4])
        early.start()
        stores.append(early)

    halves = {}

    def input_partial(k):
        shared(results[k])
        if k == 0:
            shared(q_copies)
            inputs[6].wait()
        for b in range(2):
            for ch in range(2):
                first = ab[k, 4 * b + ch].astype(F32)
                second = ab[k, 4 * b + 2 + ch].astype(F32)
                for i, out in enumerate((hid, dg, du)):
                    out[group(k) + b, :, ch * LANES : (ch + 1) * LANES] = jnp.concatenate(
                        [first[i * TB : (i + 1) * TB], second[i * TB : (i + 1) * TB]], axis=0
                    ).astype(BF16)
        def partial(block):
            part = nt(dg[block], wg[...])
            part += nt(du[block], wu[...])
            part += jnp.dot(q[block], wq[...], preferred_element_type=F32)
            return part

        gib[k] = partial(group(k) + 1 - core).astype(BF16)
        halves[k] = send(gib.at[k], cr.at[k], c_ss.at[k], c_rs.at[k], sibling)
        gif[k] = partial(group(k) + core)

    pieces = {}

    def scatter_input(k):
        halves[k].wait_recv()
        block = (gif[k] + cr[k].astype(F32)).astype(BF16)
        unpack = one_hot(NS * PAD, BLK, spreading)
        rs1[k] = (
            jnp.dot(unpack, block, preferred_element_type=F32).astype(BF16).reshape(NS, PAD, -1)
        )
        pieces[k] = [
            send(rs1.at[k, shard_peer(r)], rr1.at[k, r], r_ss.at[k, r], r_rs.at[k, r], at_s(r))
            for r in (6, 2, 5, 7, 1, 3, 4)
        ]

    ends = []

    def reduce_input(k):
        total = rs1[k, s].astype(F32)
        for copy in pieces[k]:
            copy.wait_recv()
        for r in range(1, NS):
            total = total + rr1[k, r].astype(F32)
        if k == 0:
            own[...] = total
        else:
            z2[k] = total.astype(BF16)
            ends.append(send(z2.at[k], zr.at[k], e_ss.at[k], e_rs.at[k], at_hi(k)))

    def flat(ref):
        return ref[...].reshape(NY * BLK, -1)

    gather_rows(0)
    forward_shard(1)
    pass_q()
    project(0)
    forward_shard(2)
    gather_rows(1)
    combine(0)
    project(1)
    forward_shard(3)
    elementwise(0)
    combine(1)
    gather_rows(2)
    project(2)
    pass_results(0)
    elementwise(1)
    combine(2)
    gather_rows(3)
    project(3)
    input_partial(0)
    project_grad()
    pass_results(1)
    elementwise(2)
    combine(3)
    scatter_input(0)
    input_partial(1)
    pass_results(2)
    elementwise(3)
    scatter_input(1)
    reduce_input(0)
    input_partial(2)
    pass_results(3)
    scatter_input(2)
    reduce_input(1)
    input_partial(3)
    scatter_input(3)
    reduce_input(2)
    def store(i, src, dst):
        copy = pltpu.make_async_copy(src, dst, o_sem.at[i])
        copy.start()
        stores.append(copy)

    gg_out[...] = tn(flat(xs), flat(dg)).astype(BF16)
    store(1, gg_out, gg_hbm)
    gu_out[...] = tn(flat(xs), flat(du)).astype(BF16)
    store(2, gu_out, gu_hbm)
    reduce_input(3)
    gd_out[...] = tn(flat(hid), flat(xm)).astype(BF16)
    store(3, gd_out, gd_hbm)
    total = own[...]
    for copy in ends:
        copy.wait_recv()
    for k in range(1, NH):
        total = total + zr[k].astype(F32)
    gi_out[...] = total[0:ROWS].astype(BF16)
    store(0, gi_out, gi_hbm)
    for copy in sends:
        copy.wait_send()
    for copy in stores:
        copy.wait()


def place(*refs):
    ins, outs, held = refs[:5], refs[5:10], refs[10:15]
    in_sems, out_sems = refs[15:]
    loads = [pltpu.make_async_copy(ins[i], held[i], in_sems.at[i]) for i in range(5)]
    stores = [pltpu.make_async_copy(held[i], outs[i], out_sems.at[i]) for i in range(5)]
    for copy in loads:
        copy.start()
    for load, store in zip(loads, stores):
        load.wait()
        store.start()
    for copy in stores:
        copy.wait()


def on_device(stash, mlp_grad, qkv_grad, w_gate, w_up, w_down, w_qkv):
    width = stash.shape[1]
    units = w_gate.shape[1]
    proj = w_qkv.shape[1]
    hbm = pl.BlockSpec(memory_space=pltpu.HBM)
    dma = pltpu.SemaphoreType.DMA
    results = pl.pallas_call(
        kernel,
        out_shape=(
            jax.ShapeDtypeStruct(stash.shape, BF16),
            jax.ShapeDtypeStruct(w_gate.shape, BF16),
            jax.ShapeDtypeStruct(w_up.shape, BF16),
            jax.ShapeDtypeStruct(w_down.shape, BF16),
            jax.ShapeDtypeStruct((proj, width), BF16),
        ),
        in_specs=[hbm] * 7,
        out_specs=(hbm,) * 5,
        scratch_shapes=[
            pltpu.VMEM(stash.shape, BF16),
            pltpu.VMEM(w_gate.shape, BF16),
            pltpu.VMEM(w_up.shape, BF16),
            pltpu.VMEM(w_down.shape, BF16),
            pltpu.VMEM((proj, width), BF16),
            pltpu.VMEM(stash.shape, BF16),
            pltpu.VMEM(mlp_grad.shape, BF16),
            pltpu.VMEM(qkv_grad.shape, BF16),
            pltpu.VMEM(w_gate.shape, BF16),
            pltpu.VMEM(w_up.shape, BF16),
            pltpu.VMEM(w_down.shape, BF16),
            pltpu.VMEM((proj, width), BF16),
            pltpu.VMEM((2 * PAD, width), BF16),
            pltpu.VMEM((PAD, width + 2 * LANES), BF16),
            pltpu.VMEM((NH, PAD, width + 2 * LANES), BF16),
            pltpu.VMEM((NH, NS, PAD, width + 2 * LANES), BF16),
            pltpu.VMEM((NY, BLK, width), BF16),
            pltpu.VMEM((NY, BLK, width), BF16),
            pltpu.VMEM((NY, BLK, proj), BF16),
            pltpu.VMEM((NH, NY, LANES, LANES), F32),
            pltpu.VMEM((NH, NY, LANES, LANES), BF16),
            pltpu.VMEM((NH, NY, LANES, LANES), BF16),
            pltpu.VMEM((NH, 2, LANES, LANES), BF16),
            pltpu.VMEM((NH, NY, LANES, LANES), BF16),
            pltpu.VMEM((NY, BLK, units), BF16),
            pltpu.VMEM((NY, BLK, units), BF16),
            pltpu.VMEM((NY, BLK, units), BF16),
            pltpu.VMEM((NH, BLK, width), BF16),
            pltpu.VMEM((NH, BLK, width), F32),
            pltpu.VMEM((NH, BLK, width), BF16),
            pltpu.VMEM((NH, NS, PAD, width), BF16),
            pltpu.VMEM((NH, NS, PAD, width), BF16),
            pltpu.VMEM((PAD, width), F32),
            pltpu.VMEM((NH, PAD, width), BF16),
            pltpu.VMEM((NH, PAD, width), BF16),
        ]
        + [dma((7,))]
        + [dma((5,))]
        + [dma((NH,))] * 2
        + [dma((NH, NS))] * 2
        + [dma((NH, 2))] * 2
        + [dma((NY,))] * 2
        + [dma((NH, NY))] * 2
        + [dma((NH, NY))] * 2
        + [dma((NH,))] * 2
        + [dma((NH, NS))] * 2
        + [dma((NH,))] * 2,
        compiler_params=pltpu.CompilerParams(
            collective_id=0, has_side_effects=True, vmem_limit_bytes=63 * 2**20
        ),
        cost_estimate=pl.CostEstimate(
            flops=2_600_000_000, bytes_accessed=4_000_000, transcendentals=200_000
        ),
        name="block_backward",
    )(stash, mlp_grad, qkv_grad, w_gate, w_up, w_down, w_qkv.T)
    *placed, grad_qkv = pl.pallas_call(
        place,
        out_shape=tuple(jax.ShapeDtypeStruct(a.shape, a.dtype) for a in results),
        in_specs=[hbm] * 5,
        out_specs=(hbm,) * 5,
        scratch_shapes=[pltpu.VMEM(a.shape, a.dtype) for a in results] + [dma((5,))] * 2,
        compiler_params=pltpu.CompilerParams(vmem_limit_bytes=63 * 2**20),
        name="place_results",
    )(*results)
    return (*placed, grad_qkv.T)


def solution(mesh):
    rows = P(("gy", "gz"), "gx")
    columns = P("gx", ("gy", "gz"))
    return jax.shard_map(
        on_device,
        mesh=mesh,
        in_specs=(rows, rows, columns, columns, columns, rows, columns),
        out_specs=(rows, columns, columns, rows, columns),
        check_vma=False,
    )
```

```python
import jax
import jax.numpy as jnp
from jax import lax
from jax.experimental import pallas as pl
from jax.experimental.pallas import tpu as pltpu
from jax.sharding import PartitionSpec as P

MESH = pl.DeviceIdType.MESH
F32 = jnp.float32
BF16 = jnp.bfloat16
NY = 8
NS = 8
NH = 4
ROWS = 10
PAD = 16
BLK = 80
TB = 40
LANES = 128


def nt(left, right):
    return lax.dot_general(left, right, (((1,), (1,)), ((), ())), preferred_element_type=F32)


def tn(left, right):
    return lax.dot_general(left, right, (((0,), (0,)), ((), ())), preferred_element_type=F32)


def one_hot(rows, cols, hit):
    row = lax.broadcasted_iota(jnp.int32, (rows, cols), 0)
    col = lax.broadcasted_iota(jnp.int32, (rows, cols), 1)
    return jnp.where(hit(row, col), 1.0, 0.0).astype(BF16)


def spreading(row, col):
    shard = lax.shift_right_logical(row, 4)
    token = row - shard * PAD
    return (token < ROWS) & (col == shard * ROWS + token)


def exact(left, right):
    return jnp.dot(left, right, preferred_element_type=F32)


HEAD = PAD - ROWS
TAIL = ROWS - HEAD


def pack_shard(padded, width):
    main = one_hot(PAD, 2 * PAD, lambda r, c: ((r < ROWS) & (c == r)) | ((r >= ROWS) & (c == r + HEAD)))
    parts = [exact(main, padded)]
    for half in range(2):
        part = jnp.zeros((PAD, LANES), F32)
        for i in range(4 * half, min(4 * half + 4, width // LANES)):
            low = TAIL * (i % 4)
            pick = one_hot(
                PAD, 2 * PAD, lambda r, c: (r >= low) & (r < low + TAIL) & (c == r - low + PAD + HEAD)
            )
            part += exact(pick, padded[:, i * LANES : (i + 1) * LANES])
        parts.append(part)
    return jnp.concatenate(parts, axis=1).astype(BF16)


def unpack_shards(packed, width):
    def place(row, col, low, count, start):
        shard = lax.shift_right_logical(col, 4)
        t = col - shard * PAD - low
        return (t >= 0) & (t < count) & (row == shard * ROWS + start + t)

    wide = packed[:, :width]
    rows = exact(one_hot(BLK, NS * PAD, lambda r, c: place(r, c, 0, ROWS, 0)), wide)
    grads = exact(one_hot(BLK, NS * PAD, lambda r, c: place(r, c, ROWS, HEAD, 0)), wide)
    tails = []
    for i in range(width // LANES):
        pick = one_hot(BLK, NS * PAD, lambda r, c: place(r, c, TAIL * (i % 4), TAIL, HEAD))
        first = width + LANES * (i // 4)
        tails.append(exact(pick, packed[:, first : first + LANES]))
    grads += jnp.concatenate(tails, axis=1)
    return rows.astype(BF16), grads.astype(BF16)


def kernel(
    stash_in, mlp_in, qkv_in, wg_in, wu_in, wd_in, wq_in,
    gi_hbm, gg_hbm, gu_hbm, gd_hbm, gq_hbm,
    gi_out, gg_out, gu_out, gd_out, gq_out,
    stash, mlp, qkv, wg, wu, wd, wq,
    pad, packed, zin, shards, xs, xm, q, pf, sb, rb, cb, ab, hid, dg, du, gib, gif, cr, rs1, rr1, own, z2, zr,
    w_sem, o_sem, z_ss, z_rs, g_ss, g_rs, x_ss, x_rs, q_ss, q_rs, s_ss, s_rs, a_ss, a_rs, c_ss, c_rs, r_ss, r_rs, e_ss, e_rs,
):
    y = lax.axis_index("gx")
    gy = lax.axis_index("gy")
    s = lax.axis_index("gz")
    core, hi = gy % 2, gy // 2
    lo, x = s // 4, s % 4

    def at_y(d):
        return ((y + d + NY) % NY, gy, s)

    def shard_peer(r):
        return ((lo + r // 4) % 2) * 4 + (x + r % 4) % 4

    def at_s(r):
        return (y, gy, shard_peer(r))

    def at_hi(k):
        return (y, ((hi + k + NH) % NH) * 2 + core, s)

    sibling = (y, hi * 2 + (1 - core), s)

    sends = []
    stores = []

    def send(src, dst, ss, rs, device):
        copy = pltpu.make_async_remote_copy(
            src_ref=src, dst_ref=dst, send_sem=ss, recv_sem=rs, device_id=device, device_id_type=MESH
        )
        copy.start()
        sends.append(copy)
        return copy

    inputs = [
        pltpu.make_async_copy(src, dst, w_sem.at[i])
        for i, (src, dst) in enumerate(
            (
                (stash_in, stash),
                (mlp_in, mlp),
                (qkv_in, qkv),
                (wg_in, wg),
                (wu_in, wu),
                (wd_in, wd),
                (wq_in, wq),
            )
        )
    ]
    barrier = pltpu.get_barrier_semaphore()
    partners = [at_y(d) for d in (1, -1, 2, -2)] + [at_s(r) for r in range(1, NS)]
    partners += [at_hi(k) for k in range(1, NH)] + [sibling]
    for device in partners:
        pl.semaphore_signal(barrier, inc=1, device_id=device, device_id_type=MESH)

    for copy in inputs:
        copy.start()
    for copy in inputs[:3]:
        copy.wait()
    pad[...] = jnp.zeros_like(pad)
    pad[0:ROWS, :] = stash[...]
    pad[PAD : PAD + ROWS, :] = mlp[...]
    packed[...] = pack_shard(pad[...], stash.shape[1])
    shards[0, s] = packed[...]
    q[y] = qkv[...]

    pl.semaphore_wait(barrier, len(partners))

    def spread(k, src):
        return [
            send(src, shards.at[k, s], g_ss.at[k, r], g_rs.at[k, r], at_s(r))
            for r in (6, 2, 5, 7, 1, 3, 4)
        ]

    shard_copies = {0: spread(0, packed)}
    z_copies = {
        k: send(packed, zin.at[k], z_ss.at[k], z_rs.at[k], at_hi(-k)) for k in (1, 2, 3)
    }

    def wrap(d):
        return (y + d + NY) % NY

    def share(ref, ss, rs):
        block = ref.at[y]
        return {
            d: send(block, block, ss.at[i], rs.at[i], at_y(-d))
            for i, d in enumerate((2, -2, 1, -1))
        }

    def pass_on(copies, ref, ss, rs, cut):
        halves = {2: pl.ds(0, cut), -2: pl.ds(cut, ref.shape[1] - cut)}
        for i, d in enumerate((2, -2)):
            copies[d].wait_recv()
            block = ref.at[wrap(d)]
            part = ref.at[wrap(d), halves[d]]
            sign = d // 2
            copies[2 * d] = send(part, part, ss.at[4 + i], rs.at[4 + i], at_y(-d))
            copies[d + sign] = send(block, block, ss.at[6 + i], rs.at[6 + i], at_y(-sign))

    def shared(copies):
        for d in (1, -1, 3, -3, 4, -4):
            copies[d].wait_recv()

    q_copies = share(q, q_ss, q_rs)

    def pass_q():
        pass_on(q_copies, q, q_ss, q_rs, 48)

    def group(k):
        return ((hi + k) % NH) * 2

    def forward_shard(k):
        z_copies[k].wait_recv()
        shard_copies[k] = spread(k, zin.at[k])
        shards[k, s] = zin[k]

    swaps = {}

    def gather_rows(k):
        for copy in shard_copies[k]:
            copy.wait_recv()
        block = group(k) + core
        xs[block], xm[block] = unpack_shards(shards[k].reshape(NS * PAD, -1), stash.shape[1])
        swaps[k] = [
            send(out.at[block], out.at[block], x_ss.at[k, i], x_rs.at[k, i], sibling)
            for i, out in enumerate((xs, xm))
        ]

    sums = {}

    def project(k):
        for copy in swaps[k]:
            copy.wait_recv()
        if k == 0:
            for copy in inputs[3:6]:
                copy.wait()
        rows = xs[pl.ds(group(k), 2)].reshape(2 * BLK, -1)
        grads = xm[pl.ds(group(k), 2)].reshape(2 * BLK, -1)
        gate = jnp.dot(rows, wg[...], preferred_element_type=F32)
        up = jnp.dot(rows, wu[...], preferred_element_type=F32)
        back = nt(grads, wd[...])
        for owner in range(NY):
            tb, ch = owner // 2, owner % 2
            part = jnp.concatenate(
                [
                    a[tb * TB : (tb + 1) * TB, ch * LANES : (ch + 1) * LANES]
                    for a in (gate, up, back)
                ]
                + [jnp.zeros((LANES - 3 * TB, LANES), F32)],
                axis=0,
            )
            pf[k, owner] = part
            sb[k, owner] = part.astype(BF16)
        half = {1: pl.ds(0, LANES // 2), -1: pl.ds(LANES // 2, LANES // 2)}
        sums[k] = {}
        for slot, (dist, hop) in enumerate(((4, 2), (3, 1), (1, 1))):
            for side, sign in enumerate((1, -1)):
                src = sb.at[k, wrap(sign * dist)]
                dst = rb.at[k, 2 * slot + side]
                if dist == 4:
                    src = sb.at[k, wrap(sign * dist), half[sign]]
                    dst = rb.at[k, 2 * slot + side, half[sign]]
                n = 2 * slot + side
                sums[k][dist, sign] = send(src, dst, s_ss.at[k, n], s_rs.at[k, n], at_y(sign * hop))

    def combine(k):
        for side, sign in enumerate((1, -1)):
            sums[k][4, sign].wait_recv()
            sums[k][3, sign].wait_recv()
            rows = LANES // 2 * side
            part = pf[k, wrap(2 * sign)] + rb[k, 2 + side].astype(F32)
            far = rb[k, side, rows : rows + LANES // 2, :].astype(F32)
            blank = jnp.zeros_like(far)
            part += jnp.concatenate([far, blank] if side == 0 else [blank, far], axis=0)
            cb[k, side] = part.astype(BF16)
            sums[k][2, sign] = send(
                cb.at[k, side], rb.at[k, 6 + side], s_ss.at[k, 6 + side], s_rs.at[k, 6 + side], at_y(2 * sign)
            )

    results = {}

    def elementwise(k):
        total = pf[k, y]
        for slot, dist in ((2, 1), (3, 2)):
            for side, sign in enumerate((1, -1)):
                sums[k][dist, sign].wait_recv()
                total = total + rb[k, 2 * slot + side].astype(F32)
        gate, up, back = total[0:TB], total[TB : 2 * TB], total[2 * TB : 3 * TB]
        sig = jax.nn.sigmoid(gate)
        act = gate * sig
        out = jnp.concatenate(
            [
                act * up,
                back * up * sig * (1.0 + gate * (1.0 - sig)),
                back * act,
                jnp.zeros((LANES - 3 * TB, LANES), F32),
            ],
            axis=0,
        )
        ab[k, y] = out.astype(BF16)
        results[k] = share(ab.at[k], a_ss.at[k], a_rs.at[k])

    def pass_results(k):
        pass_on(results[k], ab.at[k], a_ss.at[k], a_rs.at[k], LANES // 2)

    def project_grad():
        gq_out[...] = tn(flat(q), flat(xs)).astype(BF16)
        early = pltpu.make_async_copy(gq_out, gq_hbm, o_sem.at[4])
        early.start()
        stores.append(early)

    halves = {}

    def input_partial(k):
        shared(results[k])
        if k == 0:
            shared(q_copies)
            inputs[6].wait()
        for b in range(2):
            for ch in range(2):
                first = ab[k, 4 * b + ch].astype(F32)
                second = ab[k, 4 * b + 2 + ch].astype(F32)
                for i, out in enumerate((hid, dg, du)):
                    out[group(k) + b, :, ch * LANES : (ch + 1) * LANES] = jnp.concatenate(
                        [first[i * TB : (i + 1) * TB], second[i * TB : (i + 1) * TB]], axis=0
                    ).astype(BF16)
        def partial(block):
            part = nt(dg[block], wg[...])
            part += nt(du[block], wu[...])
            part += jnp.dot(q[block], wq[...], preferred_element_type=F32)
            return part

        gib[k] = partial(group(k) + 1 - core).astype(BF16)
        halves[k] = send(gib.at[k], cr.at[k], c_ss.at[k], c_rs.at[k], sibling)
        gif[k] = partial(group(k) + core)

    pieces = {}

    def scatter_input(k):
        halves[k].wait_recv()
        block = (gif[k] + cr[k].astype(F32)).astype(BF16)
        unpack = one_hot(NS * PAD, BLK, spreading)
        rs1[k] = (
            jnp.dot(unpack, block, preferred_element_type=F32).astype(BF16).reshape(NS, PAD, -1)
        )
        pieces[k] = [
            send(rs1.at[k, shard_peer(r)], rr1.at[k, r], r_ss.at[k, r], r_rs.at[k, r], at_s(r))
            for r in (6, 2, 5, 7, 1, 3, 4)
        ]

    ends = []

    def reduce_input(k):
        total = rs1[k, s].astype(F32)
        for copy in pieces[k]:
            copy.wait_recv()
        for r in range(1, NS):
            total = total + rr1[k, r].astype(F32)
        if k == 0:
            own[...] = total
        else:
            z2[k] = total.astype(BF16)
            ends.append(send(z2.at[k], zr.at[k], e_ss.at[k], e_rs.at[k], at_hi(k)))

    def flat(ref):
        return ref[...].reshape(NY * BLK, -1)

    gather_rows(0)
    forward_shard(1)
    pass_q()
    project(0)
    forward_shard(2)
    gather_rows(1)
    combine(0)
    project(1)
    forward_shard(3)
    elementwise(0)
    combine(1)
    gather_rows(2)
    project(2)
    pass_results(0)
    elementwise(1)
    combine(2)
    gather_rows(3)
    project(3)
    input_partial(0)
    project_grad()
    pass_results(1)
    elementwise(2)
    combine(3)
    scatter_input(0)
    input_partial(1)
    pass_results(2)
    elementwise(3)
    scatter_input(1)
    reduce_input(0)
    input_partial(2)
    pass_results(3)
    scatter_input(2)
    reduce_input(1)
    input_partial(3)
    scatter_input(3)
    reduce_input(2)
    def store(i, src, dst):
        copy = pltpu.make_async_copy(src, dst, o_sem.at[i])
        copy.start()
        stores.append(copy)

    gg_out[...] = tn(flat(xs), flat(dg)).astype(BF16)
    store(1, gg_out, gg_hbm)
    gu_out[...] = tn(flat(xs), flat(du)).astype(BF16)
    store(2, gu_out, gu_hbm)
    reduce_input(3)
    gd_out[...] = tn(flat(hid), flat(xm)).astype(BF16)
    store(3, gd_out, gd_hbm)
    total = own[...]
    for copy in ends:
        copy.wait_recv()
    for k in range(1, NH):
        total = total + zr[k].astype(F32)
    gi_out[...] = total[0:ROWS].astype(BF16)
    store(0, gi_out, gi_hbm)
    for copy in sends:
        copy.wait_send()
    for copy in stores:
        copy.wait()


def place(*refs):
    ins, outs, held = refs[:5], refs[5:10], refs[10:15]
    in_sems, out_sems = refs[15:]
    loads, stores = [], []
    for i in range(5):
        rows = ins[i].shape[0]
        cuts = (0, rows) if rows < 2 * PAD else (0, rows // 2, rows)
        for h in range(len(cuts) - 1):
            part = pl.ds(cuts[h], cuts[h + 1] - cuts[h])
            loads.append(pltpu.make_async_copy(ins[i].at[part], held[i].at[part], in_sems.at[i, h]))
            stores.append(pltpu.make_async_copy(held[i].at[part], outs[i].at[part], out_sems.at[i, h]))
    for copy in loads:
        copy.start()
    for load, store in zip(loads, stores):
        load.wait()
        store.start()
    for copy in stores:
        copy.wait()


def on_device(stash, mlp_grad, qkv_grad, w_gate, w_up, w_down, w_qkv):
    width = stash.shape[1]
    units = w_gate.shape[1]
    proj = w_qkv.shape[1]
    hbm = pl.BlockSpec(memory_space=pltpu.HBM)
    dma = pltpu.SemaphoreType.DMA
    results = pl.pallas_call(
        kernel,
        out_shape=(
            jax.ShapeDtypeStruct(stash.shape, BF16),
            jax.ShapeDtypeStruct(w_gate.shape, BF16),
            jax.ShapeDtypeStruct(w_up.shape, BF16),
            jax.ShapeDtypeStruct(w_down.shape, BF16),
            jax.ShapeDtypeStruct((proj, width), BF16),
        ),
        in_specs=[hbm] * 7,
        out_specs=(hbm,) * 5,
        scratch_shapes=[
            pltpu.VMEM(stash.shape, BF16),
            pltpu.VMEM(w_gate.shape, BF16),
            pltpu.VMEM(w_up.shape, BF16),
            pltpu.VMEM(w_down.shape, BF16),
            pltpu.VMEM((proj, width), BF16),
            pltpu.VMEM(stash.shape, BF16),
            pltpu.VMEM(mlp_grad.shape, BF16),
            pltpu.VMEM(qkv_grad.shape, BF16),
            pltpu.VMEM(w_gate.shape, BF16),
            pltpu.VMEM(w_up.shape, BF16),
            pltpu.VMEM(w_down.shape, BF16),
            pltpu.VMEM((proj, width), BF16),
            pltpu.VMEM((2 * PAD, width), BF16),
            pltpu.VMEM((PAD, width + 2 * LANES), BF16),
            pltpu.VMEM((NH, PAD, width + 2 * LANES), BF16),
            pltpu.VMEM((NH, NS, PAD, width + 2 * LANES), BF16),
            pltpu.VMEM((NY, BLK, width), BF16),
            pltpu.VMEM((NY, BLK, width), BF16),
            pltpu.VMEM((NY, BLK, proj), BF16),
            pltpu.VMEM((NH, NY, LANES, LANES), F32),
            pltpu.VMEM((NH, NY, LANES, LANES), BF16),
            pltpu.VMEM((NH, NY, LANES, LANES), BF16),
            pltpu.VMEM((NH, 2, LANES, LANES), BF16),
            pltpu.VMEM((NH, NY, LANES, LANES), BF16),
            pltpu.VMEM((NY, BLK, units), BF16),
            pltpu.VMEM((NY, BLK, units), BF16),
            pltpu.VMEM((NY, BLK, units), BF16),
            pltpu.VMEM((NH, BLK, width), BF16),
            pltpu.VMEM((NH, BLK, width), F32),
            pltpu.VMEM((NH, BLK, width), BF16),
            pltpu.VMEM((NH, NS, PAD, width), BF16),
            pltpu.VMEM((NH, NS, PAD, width), BF16),
            pltpu.VMEM((PAD, width), F32),
            pltpu.VMEM((NH, PAD, width), BF16),
            pltpu.VMEM((NH, PAD, width), BF16),
        ]
        + [dma((7,))]
        + [dma((5,))]
        + [dma((NH,))] * 2
        + [dma((NH, NS))] * 2
        + [dma((NH, 2))] * 2
        + [dma((NY,))] * 2
        + [dma((NH, NY))] * 2
        + [dma((NH, NY))] * 2
        + [dma((NH,))] * 2
        + [dma((NH, NS))] * 2
        + [dma((NH,))] * 2,
        compiler_params=pltpu.CompilerParams(
            collective_id=0, has_side_effects=True, vmem_limit_bytes=63 * 2**20
        ),
        cost_estimate=pl.CostEstimate(
            flops=2_600_000_000, bytes_accessed=4_000_000, transcendentals=200_000
        ),
        name="block_backward",
    )(stash, mlp_grad, qkv_grad, w_gate, w_up, w_down, w_qkv.T)
    *placed, grad_qkv = pl.pallas_call(
        place,
        out_shape=tuple(jax.ShapeDtypeStruct(a.shape, a.dtype) for a in results),
        in_specs=[hbm] * 5,
        out_specs=(hbm,) * 5,
        scratch_shapes=[pltpu.VMEM(a.shape, a.dtype) for a in results] + [dma((5, 2))] * 2,
        compiler_params=pltpu.CompilerParams(vmem_limit_bytes=63 * 2**20),
        name="place_results",
    )(*results)
    return (*placed, grad_qkv.T)


def solution(mesh):
    rows = P(("gy", "gz"), "gx")
    columns = P("gx", ("gy", "gz"))
    return jax.shard_map(
        on_device,
        mesh=mesh,
        in_specs=(rows, rows, columns, columns, columns, rows, columns),
        out_specs=(rows, columns, columns, rows, columns),
        check_vma=False,
    )
```
